128 devices in a mesh: dp: 2 (over core), ctx: 16 (over y, x), fsdp: 4 (over z).
Axes of the slice: x: 4, y: 4, z: 4, core: 2. Of those that a mesh axis runs over, the one named last changes fastest.
Arguments:
- tokens: bfloat16 [8, 3072, 896], P(('dp', 'fsdp'), 'ctx'), may hold values from -6 to 6
- norm_attn: bfloat16 [896], P('fsdp'), may hold values from 0.5 to 1.5
- w_qkv: bfloat16 [896, 1152], P('fsdp'), may hold values from -0.1875 to 0.1875
- b_qkv: bfloat16 [1152], P('fsdp'), may hold values from -3 to 3
- w_out: bfloat16 [896, 896], P('fsdp'), may hold values from -1 to 1
- norm_mlp: bfloat16 [896], P('fsdp'), may hold values from 0.5 to 1.5
- w_gate: bfloat16 [896, 4864], P('fsdp'), may hold values from -0.1875 to 0.1875
- w_up: bfloat16 [896, 4864], P('fsdp'), may hold values from -0.1875 to 0.1875
- w_down: bfloat16 [4864, 896], P('fsdp'), may hold values from -0.078125 to 0.078125
- cotangent: bfloat16 [8, 3072, 896], P(('dp', 'fsdp'), 'ctx'), may hold values from -6 to 6
Outputs:
- layer_out: bfloat16 [8, 3072, 896], P(('dp', 'fsdp'), 'ctx')
- grad_tokens: bfloat16 [8, 3072, 896], P(('dp', 'fsdp'), 'ctx')
- grad_norm_attn: float32 [896], P('fsdp')
- grad_w_qkv: float32 [896, 1152], P('fsdp')
- grad_b_qkv: float32 [1024], P('fsdp')
- grad_b_value: float32 [128], P('fsdp')
- grad_w_out: float32 [896, 896], P('fsdp')
- grad_norm_mlp: float32 [896], P('fsdp')
- grad_w_gate: float32 [896, 4864], P('fsdp')
- grad_w_up: float32 [896, 4864], P('fsdp')
- grad_w_down: float32 [4864, 896], P('fsdp')
The draws below stay inside these ranges and needn't reach their ends.
All inputs are finite; a program needn't handle non-finite values.
Results may differ from the reference program's by a relative error of at most 0.03.
Values may be sent and summed in bfloat16 or wider, within the bound.
No kernel may reach another device: no remote copies, remote signals or barrier semaphores. Data moves between devices by JAX's collectives and lax.ppermute only.
A program may use at most 256 MiB of HBM per device.

```python
import math
import jax
import jax.numpy as jnp
from jax import lax

D = 896
HEADS = 14
KV = 2
HD = 64
FF = 4864
QKV = 1152
LEN = 3072
SEQS = 8


def levels(rng, extent, split, low, top_value):
    gain, own = 1.0, jax.random.fold_in(rng, 6)
    for dim, shards_of in split:
        steps = jnp.exp(jax.random.uniform(jax.random.fold_in(own, dim), (shards_of,), jnp.float32, low / len(split), top_value / len(split)))
        gain = gain * jnp.repeat(steps, extent[dim] // shards_of).reshape([-1 if axis == dim else 1 for axis in range(len(extent))])
    return gain


def centred(own_key, dims, deviation, most, pieces=(), kind=jnp.bfloat16):
    values = deviation * jax.random.normal(own_key, dims, jnp.float32)
    if pieces:
        values = values * levels(own_key, dims, pieces, -0.22, 0.18)
    return jnp.clip(values, -most, most).astype(kind)


def setup_inputs(seed: int = 0) -> dict:
    arg_keys = jax.random.split(jax.random.key(seed), 11)
    return {
        "tokens": centred(arg_keys[0], (SEQS, LEN, D), 1.0, 6.0, ((0, 8), (1, 16))),
        "norm_attn": jnp.clip(1.0 + 0.1 * jax.random.normal(arg_keys[1], (D,), jnp.float32), 0.5, 1.5).astype(jnp.bfloat16),
        "w_qkv": centred(arg_keys[2], (D, QKV), D ** -0.5, 0.1875, ((0, 4),)),
        "b_qkv": centred(arg_keys[3], (QKV,), 0.5, 3.0, ((0, 4),)),
        "w_out": centred(arg_keys[4], (D, D), (D // 32) ** -0.5, 1.0, ((0, 4),)),
        "norm_mlp": jnp.clip(1.0 + 0.1 * jax.random.normal(arg_keys[5], (D,), jnp.float32), 0.5, 1.5).astype(jnp.bfloat16),
        "w_gate": centred(arg_keys[6], (D, FF), D ** -0.5, 0.1875, ((0, 4),)),
        "w_up": centred(arg_keys[7], (D, FF), D ** -0.5, 0.1875, ((0, 4),)),
        "w_down": centred(arg_keys[8], (FF, D), FF ** -0.5, 0.078125, ((0, 4),)),
        "cotangent": centred(arg_keys[9], (SEQS, LEN, D), 1.0, 6.0, ((0, 8), (1, 16))),
    }


NORM_EPS = 1e-06
ROPE_THETA = 1000000.0
MASK_VALUE = -1e+30

@jax.custom_vjp
def low(v):
    return lax.optimization_barrier(v.astype(jnp.bfloat16)).astype(jnp.float32)

@jax.custom_vjp
def low_back(v):
    return v

def low_keep(v):
    return (low(v), None)

def low_pass(kept, grad):
    return (grad,)

def back_keep(v):
    return (v, None)

def back_low(kept, grad):
    return (low(grad),)
low.defvjp(low_keep, low_pass)
low_back.defvjp(back_keep, back_low)

def product(left, right):
    return jnp.dot(left, right, precision=lax.Precision.HIGHEST, preferred_element_type=jnp.float32)

def rope_tables(positions, head_size):
    half_size = head_size // 2
    frequency = ROPE_THETA ** (-jnp.arange(half_size, dtype=jnp.float32) * 2.0 / head_size)
    angles = positions.astype(jnp.float32)[:, None] * frequency[None, :]
    return (jnp.cos(angles), jnp.sin(angles))

def rotate(values, cosine, sine_table):
    half_size = values.shape[-1] // 2
    first_half = values[..., :half_size]
    second_half = values[..., half_size:]
    cos_rows = cosine[:, None, :]
    sin_rows = sine_table[:, None, :]
    return jnp.concatenate([first_half * cos_rows - second_half * sin_rows, second_half * cos_rows + first_half * sin_rows], -1)

def normalize(values, gain_row):
    return values * lax.rsqrt(lax.optimization_barrier(jnp.mean(values * values, -1, keepdims=True)) + NORM_EPS) * gain_row

def attention(queries, key_rows, value_rows):
    length = queries.shape[0]
    block_size = math.gcd(512, length)
    groups = HEADS // KV
    score_scale = HD ** (-0.5)
    query_blocks = queries.reshape(length // block_size, block_size, KV, groups, HD)
    first_rows = jnp.arange(length // block_size, dtype=jnp.int32) * block_size
    key_index = jnp.arange(length, dtype=jnp.int32)

    def one_block(inputs):
        query_block, first_row = inputs
        raw_scores = jnp.einsum('qjgd,kjd->jgqk', query_block, key_rows, precision=lax.Precision.HIGHEST) * score_scale
        query_index = first_row + jnp.arange(block_size, dtype=jnp.int32)
        allowed = key_index[None, :] <= query_index[:, None]
        scores = low_back(jnp.where(allowed, raw_scores, MASK_VALUE))
        row_max = lax.optimization_barrier(jnp.max(scores, -1, keepdims=True))
        exp_scores = jnp.exp(scores - row_max)
        probs_block = exp_scores / lax.optimization_barrier(jnp.sum(exp_scores, -1, keepdims=True))
        mixed_heads = jnp.einsum('jgqk,kjd->qjgd', low(probs_block), value_rows, precision=lax.Precision.HIGHEST)
        return mixed_heads.reshape(block_size, HEADS * HD)
    attended = lax.map(jax.checkpoint(one_block), (query_blocks, first_rows))
    return attended.reshape(length, HEADS * HD)

def layer(hidden_in, norm_attn, w_qkv, b_qkv, w_out, norm_mlp, w_gate, w_up, w_down):
    length = hidden_in.shape[0]
    q_width = HEADS * HD
    kv_width = KV * HD
    cosine, sine_table = rope_tables(jnp.arange(length, dtype=jnp.int32), HD)
    normed_attn = low(normalize(hidden_in, norm_attn))
    projected = low_back(product(normed_attn, w_qkv) + b_qkv)
    queries = low(rotate(projected[:, :q_width].reshape(length, HEADS, HD), cosine, sine_table))
    key_rows = low(rotate(projected[:, q_width:q_width + kv_width].reshape(length, KV, HD), cosine, sine_table))
    value_rows = low(projected[:, q_width + kv_width:].reshape(length, KV, HD))
    attended = low(low_back(attention(queries, key_rows, value_rows)))
    hidden_mid = hidden_in + low_back(product(attended, w_out))
    normed_mlp = low(normalize(hidden_mid, norm_mlp))
    gate_act = low_back(product(normed_mlp, w_gate))
    up_act = low_back(product(normed_mlp, w_up))
    mixed = low(gate_act * jax.nn.sigmoid(gate_act) * up_act)
    return hidden_mid + low_back(product(mixed, w_down))

def reference(tokens, norm_attn, w_qkv, b_qkv, w_out, norm_mlp, w_gate, w_up, w_down, cotangent):

    def forward(inputs, gain_one, qkv_weight, qkv_bias, out_weight, gain_two, gate_weight, up_weight, down_weight):

        def one_sequence(sequence):
            return layer(sequence, gain_one, qkv_weight, qkv_bias, out_weight, gain_two, gate_weight, up_weight, down_weight)
        return lax.map(jax.checkpoint(one_sequence), inputs)
    outputs, pullback = jax.vjp(forward, tokens.astype(jnp.float32), norm_attn.astype(jnp.float32), w_qkv.astype(jnp.float32), b_qkv.astype(jnp.float32), w_out.astype(jnp.float32), norm_mlp.astype(jnp.float32), w_gate.astype(jnp.float32), w_up.astype(jnp.float32), w_down.astype(jnp.float32))
    grads_all = pullback(cotangent.astype(jnp.float32))
    qk_cols = (HEADS + KV) * HD
    bias_grad = grads_all[3]
    return (outputs.astype(jnp.bfloat16), grads_all[0].astype(jnp.bfloat16), grads_all[1], grads_all[2], bias_grad[:qk_cols], bias_grad[qk_cols:], grads_all[4], grads_all[5], grads_all[6], grads_all[7], grads_all[8])
```

```python
import jax
import jax.numpy as jnp
from jax import lax
from jax.experimental import pallas as pl
from jax.experimental.pallas import tpu as pltpu
from jax.sharding import Mesh, PartitionSpec as P

HEADS = 14
KV = 2
HD = 64
GROUPS = HEADS // KV
RING = 4
KEY_BLOCK = 512

NORM_EPS = 1e-06
ROPE_THETA = 1000000.0
MASK_VALUE = -1e30

NT = (((1,), (1,)), ((), ()))
NN = (((1,), (0,)), ((), ()))
TN = (((0,), (0,)), ((), ()))
F32 = jnp.float32
BF16 = jnp.bfloat16


def dotf(a,b,dims): return lax.dot_general(a,b,dims,preferred_element_type=jnp.float32)

def key_loops(first_row, tok, key_count, step):
    full=lax.div(first_row,KEY_BLOCK)
    used=jnp.minimum(lax.div(first_row+(tok+KEY_BLOCK-1),KEY_BLOCK), key_count//KEY_BLOCK)
    def plain(i,_):
        step(i,False); return 0
    def masked(i,_):
        step(i,True); return 0
    lax.fori_loop(0,full,plain,0)
    lax.fori_loop(full,used,masked,0)
    return used

def stack_heads(src_ref, dst_ref, tok):
    for h in range(HEADS):
        j,g=divmod(h,GROUPS)
        dst_ref[j,g*tok:(g+1)*tok,:]=src_ref[:,h*HD:(h+1)*HD]

def unstack_heads(cols, out_ref, tok, cast):
    for pair in range(HEADS//2):
        two=[]
        for h in (2*pair,2*pair+1):
            j,g=divmod(h,GROUPS)
            two.append(cols[j][:,g*tok:(g+1)*tok])
        out_ref[:,pair*2*HD:(pair+1)*2*HD]=jnp.concatenate(two,0).T.astype(cast)

def mask_scores(s, row_ref, start):
    keys=start+lax.broadcasted_iota(jnp.int32,s.shape,0)
    return jnp.where(keys<=row_ref[0:1,:],s,MASK_VALUE)

def fwd_kernel(first_ref, q_ref, kv_ref, row_ref, o_ref, lse_ref, qs, m_s, acc):
    tok=q_ref.shape[0]
    stack_heads(q_ref,qs,tok)
    m_s[...]=jnp.full(m_s.shape,MASK_VALUE,jnp.float32)
    acc[...]=jnp.zeros(acc.shape,jnp.float32)
    def step(i,masked):
        start=pl.multiple_of(i*KEY_BLOCK,KEY_BLOCK)
        kv=kv_ref[pl.ds(start,KEY_BLOCK),:]
        for j in range(KV):
            k=kv[:,j*HD:(j+1)*HD]; v=kv[:,(KV+j)*HD:(KV+j+1)*HD]
            s=dotf(k,qs[j],NT)
            if masked: s=mask_scores(s,row_ref,start)
            m_old=m_s[j,0:1,:]
            m_new=jnp.maximum(m_old,jnp.max(s,0,keepdims=True))
            p=jnp.exp(s-m_new)
            vx=jnp.concatenate([v,jnp.ones((KEY_BLOCK,HD),jnp.bfloat16)],1)
            acc[j]=acc[j]*jnp.exp(m_old-m_new)+dotf(vx,p.astype(jnp.bfloat16),TN)[:HD+8]
            m_s[j,0:1,:]=m_new
    key_loops(first_ref[0],tok,kv_ref.shape[0],step)
    cols=[]
    for j in range(KV):
        total=acc[j,HD:HD+1,:]
        cols.append(acc[j,:HD,:]/total)
        lse_ref[j,:,:]=jnp.broadcast_to(m_s[j,0:1,:]+jnp.log(total),lse_ref.shape[1:])
    unstack_heads(cols,o_ref,tok,o_ref.dtype)

def bwd_kernel(first_ref, q_ref, kv_ref, row_ref, do_ref, o_ref, lse_ref, dq_ref, dkv_ref, qs, dos, delta_s, dq_s):
    tok=q_ref.shape[0]
    stack_heads(q_ref,qs,tok)
    stack_heads(do_ref,dos,tok)
    prod=do_ref[...].astype(jnp.float32)*o_ref[...].astype(jnp.float32)
    ones=jnp.ones((8,HD),jnp.float32)
    for h in range(HEADS):
        j,g=divmod(h,GROUPS)
        delta_s[j,:,g*tok:(g+1)*tok]=lax.dot_general(ones,prod[:,h*HD:(h+1)*HD],NT,precision=lax.Precision.HIGHEST,preferred_element_type=jnp.float32)
    dq_s[...]=jnp.zeros(dq_s.shape,jnp.float32)
    def step(i,masked):
        start=pl.multiple_of(i*KEY_BLOCK,KEY_BLOCK)
        kv=kv_ref[pl.ds(start,KEY_BLOCK),:]
        dk=[];dv=[]
        for j in range(KV):
            k=kv[:,j*HD:(j+1)*HD]; v=kv[:,(KV+j)*HD:(KV+j+1)*HD]
            s=dotf(k,qs[j],NT)
            if masked: s=mask_scores(s,row_ref,start)
            p=jnp.exp(s-lse_ref[j,0:1,:])
            dp=dotf(v,dos[j],NT)
            ds=(p*(dp-delta_s[j,0:1,:])).astype(jnp.bfloat16)
            dv.append(dotf(p.astype(jnp.bfloat16),dos[j],NN))
            dk.append(dotf(ds,qs[j],NN))
            dq_s[j]+=dotf(k,ds,TN)
        dkv_ref[pl.ds(start,KEY_BLOCK),:]=jnp.concatenate(dk+dv,1).astype(dkv_ref.dtype)
    used=key_loops(first_ref[0],tok,kv_ref.shape[0],step)
    def clear(i,_):
        dkv_ref[pl.ds(pl.multiple_of(i*KEY_BLOCK,KEY_BLOCK),KEY_BLOCK),:]=jnp.zeros((KEY_BLOCK,dkv_ref.shape[1]),dkv_ref.dtype)
        return 0
    lax.fori_loop(used,kv_ref.shape[0]//KEY_BLOCK,clear,0)
    unstack_heads([dq_s[j]*(HD**-0.5) for j in range(KV)],dq_ref,tok,dq_ref.dtype)

VM=pl.BlockSpec(memory_space=pltpu.VMEM)
SM=pl.BlockSpec(memory_space=pltpu.SMEM)
def attention_forward(first,q,kv,row_pos):
    tok=q.shape[0]; rows=GROUPS*tok
    return pl.pallas_call(fwd_kernel,
        out_shape=(jax.ShapeDtypeStruct((tok,HEADS*HD),jnp.bfloat16),jax.ShapeDtypeStruct((KV,8,rows),jnp.float32)),
        in_specs=[SM,VM,VM,VM],out_specs=(VM,VM),
        scratch_shapes=[pltpu.VMEM((KV,rows,HD),jnp.bfloat16),pltpu.VMEM((KV,8,rows),jnp.float32),pltpu.VMEM((KV,HD+8,rows),jnp.float32)],
        compiler_params=pltpu.CompilerParams(vmem_limit_bytes=48*2**20),
        cost_estimate=pl.CostEstimate(flops=2*2*HEADS*tok*kv.shape[0]*HD*4,bytes_accessed=3*2**20,transcendentals=HEADS*tok*kv.shape[0]),
    )(first,q,kv,row_pos)
def attention_backward(first,q,kv,row_pos,do,o,lse):
    tok=q.shape[0]; rows=GROUPS*tok
    return pl.pallas_call(bwd_kernel,
        out_shape=(jax.ShapeDtypeStruct((tok,HEADS*HD),jnp.float32),jax.ShapeDtypeStruct(kv.shape,jnp.bfloat16)),
        in_specs=[SM]+[VM]*6,out_specs=(VM,VM),
        scratch_shapes=[pltpu.VMEM((KV,rows,HD),jnp.bfloat16),pltpu.VMEM((KV,rows,HD),jnp.bfloat16),pltpu.VMEM((KV,8,rows),jnp.float32),pltpu.VMEM((KV,HD,rows),jnp.float32)],
        compiler_params=pltpu.CompilerParams(vmem_limit_bytes=48*2**20),
        cost_estimate=pl.CostEstimate(flops=5*2*HEADS*tok*kv.shape[0]*HD*4,bytes_accessed=5*2**20,transcendentals=HEADS*tok*kv.shape[0]),
    )(first,q,kv,row_pos,do,o,lse)


def rope_tables(positions, head_size):
    half_size = head_size // 2
    frequency = ROPE_THETA ** (-jnp.arange(half_size, dtype=jnp.float32) * 2.0 / head_size)
    angles = positions.astype(jnp.float32)[:, None] * frequency[None, :]
    return (jnp.cos(angles), jnp.sin(angles))


def rotate(values, cosine, sine_table):
    tok, width = values.shape
    values = values.reshape(tok, width // HD, HD)
    half_size = HD // 2
    first_half = values[..., :half_size]
    second_half = values[..., half_size:]
    cos_rows = cosine[:, None, :]
    sin_rows = sine_table[:, None, :]
    return jnp.concatenate(
        [
            first_half * cos_rows - second_half * sin_rows,
            second_half * cos_rows + first_half * sin_rows,
        ],
        -1,
    ).reshape(tok, width)


def inverse_rms(values):
    return lax.rsqrt(jnp.mean(values * values, -1, keepdims=True) + NORM_EPS)


def norm_back(grad_rows, values, row_scale, gain_row):
    grad_normed = grad_rows * gain_row
    cubed = row_scale * row_scale * row_scale
    grad_values = row_scale * grad_normed - values * cubed * jnp.mean(
        grad_normed * values, -1, keepdims=True
    )
    grad_gain = jnp.sum(grad_rows * values * row_scale, 0)
    return (grad_values, grad_gain)


def dot(left, right, dims=NN):
    return lax.dot_general(left, right, dims, preferred_element_type=F32)


def shift(values, axis, step):
    return lax.ppermute(values, axis, [(i, (i + step) % RING) for i in range(RING)])


def swap(values):
    return lax.ppermute(values, "dp", [(0, 1), (1, 0)])


def pick(values, index, axis=0):
    return lax.dynamic_index_in_dim(values, index, axis, keepdims=False)


def place(parts, where, axis=0):
    shape = list(parts[0].shape)
    shape.insert(axis, len(parts))
    whole = jnp.zeros(shape, parts[0].dtype)
    for part, slot in zip(parts, where):
        whole = lax.dynamic_update_index_in_dim(whole, part, slot, axis)
    return whole


def ring_gather(values, axis, me):
    parts = [values] + [shift(values, axis, k) for k in (1, 2, 3)]
    return place(parts, [(me - k) % RING for k in range(RING)])


def ring_blocks(values, axis):
    return jnp.concatenate([values] + [shift(values, axis, k) for k in (1, 2, 3)], 0)


def ring_return(parts, axis):
    total = parts[0].astype(F32)
    for k in (1, 2, 3):
        total = total + shift(parts[k].astype(BF16), axis, -k).astype(F32)
    return total


def ring_scatter(parts, axis, me):
    total = pick(parts, me).astype(F32)
    for k in (1, 2, 3):
        total = total + shift(pick(parts, (me + k) % RING).astype(BF16), axis, k).astype(F32)
    return total


def pair_scatter(parts, dp):
    mine = pick(parts, dp, 1).astype(F32)
    return mine + swap(pick(parts, 1 - dp, 1).astype(BF16)).astype(F32)


def pair_gather(values, dp, axis):
    return place([values, swap(values)], [dp, 1 - dp], axis)


def per_device(tokens, norm_attn, w_qkv, b_qkv, w_out, norm_mlp, w_gate, w_up, w_down, cotangent):
    tok = tokens.shape[1]
    width = tokens.shape[2]
    part = norm_attn.shape[0]
    q_width = HEADS * HD
    kv_width = KV * HD
    qk_width = q_width + kv_width
    qkv_width = w_qkv.shape[1]
    bias_part = b_qkv.shape[0]
    hidden_part = w_down.shape[0]
    half_part = part // 2
    dp = lax.axis_index("dp")
    yi = lax.axis_index("y")
    xi = lax.axis_index("x")
    zi = lax.axis_index("fsdp")
    hidden_in = tokens[0].astype(F32)
    grad_out = cotangent[0]
    first = (yi * RING + xi) * tok
    positions = first + jnp.arange(tok, dtype=jnp.int32)
    row_pos = jnp.broadcast_to(jnp.tile(positions, GROUPS)[None], (8, GROUPS * tok))
    first_row = first.astype(jnp.int32)[None]
    cosine, sine_table = rope_tables(positions, HD)

    small = jnp.concatenate([norm_attn, b_qkv, norm_mlp])
    small_rows = 16
    small = jnp.pad(small, (0, small_rows * 2 * kv_width - small.shape[0]))
    first_weights = lax.all_gather(
        jnp.concatenate([w_qkv[:, q_width:], small.reshape(small_rows, 2 * kv_width)], 0),
        "fsdp",
        axis=0,
    )
    w_kv = first_weights[:, :part].reshape(width, 2 * kv_width)
    vectors = first_weights[:, part:].reshape(RING, small_rows * 2 * kv_width)
    gain_attn = vectors[:, :part].reshape(-1).astype(F32)
    bias = vectors[:, part : part + bias_part].reshape(-1).astype(F32)
    gain_mlp = vectors[:, part + bias_part : 2 * part + bias_part].reshape(-1).astype(F32)
    w_query = lax.all_gather(w_qkv[:, :q_width], "fsdp", axis=0, tiled=True)
    full_out = lax.all_gather(w_out, "fsdp", axis=0, tiled=True)

    scale_attn = inverse_rms(hidden_in)
    normed_attn = (hidden_in * scale_attn * gain_attn).astype(BF16)
    proj_kv = dot(normed_attn, w_kv) + bias[q_width:]
    key_local = rotate(proj_kv[:, :kv_width], cosine, sine_table).astype(BF16)
    kv_local = jnp.concatenate([key_local, proj_kv[:, kv_width:].astype(BF16)], 1)
    kv_row = ring_gather(kv_local, "x", xi).reshape(RING * tok, 2 * kv_width)
    kv_all = ring_gather(kv_row, "y", yi).reshape(RING * RING * tok, 2 * kv_width)

    query = rotate(dot(normed_attn, w_query) + bias[:q_width], cosine, sine_table).astype(BF16)
    query = query * jnp.asarray(HD**-0.5, BF16)

    grad_out_group = ring_blocks(grad_out, "fsdp")
    both = jnp.stack(
        [lax.dynamic_slice_in_dim(w, dp * half_part, half_part, 0) for w in (w_gate, w_up)]
    )
    pieces = []
    for k in range(RING):
        cut = lax.dynamic_slice_in_dim(both, ((zi + k) % RING) * hidden_part, hidden_part, 2)
        pieces.append(shift(cut, "fsdp", k) if k else cut)
    both = place(pieces, [(zi - k) % RING for k in range(RING)], 1)
    both = pair_gather(both, dp, 2).reshape(2, width, hidden_part)
    full_gate, full_up = both[0], both[1]

    attn_low, log_total = attention_forward(first_row, query, kv_all, row_pos)
    hidden_mid = hidden_in + dot(attn_low, full_out)
    scale_mlp = inverse_rms(hidden_mid)
    normed_mlp = (hidden_mid * scale_mlp * gain_mlp).astype(BF16)
    normed_group = ring_blocks(normed_mlp, "fsdp")
    gate_act = dot(normed_group, full_gate)
    up_act = dot(normed_group, full_up)
    sigmoid_gate = jax.nn.sigmoid(gate_act)
    silu_gate = gate_act * sigmoid_gate
    mixed = (silu_gate * up_act).astype(BF16)
    grad_mixed = dot(grad_out_group, w_down, NT)
    grad_gate_low = (
        grad_mixed * up_act * sigmoid_gate * (1.0 + gate_act * (1.0 - sigmoid_gate))
    ).astype(BF16)
    grad_up_low = (grad_mixed * silu_gate).astype(BF16)
    grad_normed_part = dot(grad_gate_low, full_gate, NT) + dot(grad_up_low, full_up, NT)
    grad_normed_mlp = ring_return(grad_normed_part.reshape(RING, tok, width), "fsdp")
    out_part = dot(mixed, w_down).astype(BF16)
    layer_out = (hidden_mid + ring_return(out_part.reshape(RING, tok, width), "fsdp")).astype(BF16)

    grad_mid_norm, grad_gain_mlp = norm_back(grad_normed_mlp, hidden_mid, scale_mlp, gain_mlp)
    grad_mid = grad_out.astype(F32) + grad_mid_norm
    grad_branch = grad_mid.astype(BF16)

    grad_down_w = dot(mixed, grad_out_group, TN).astype(BF16)
    grad_both_w = jnp.stack(
        [dot(normed_group, g, TN).astype(BF16) for g in (grad_gate_low, grad_up_low)]
    )
    down_half = pair_scatter(grad_down_w.reshape(1, 2, hidden_part // 2, width), dp)[0].astype(BF16)
    both_half = pair_scatter(
        grad_both_w.reshape(2 * RING, 2, half_part, hidden_part), dp
    ).astype(BF16).reshape(2, RING, half_part, hidden_part)
    both_cols = jnp.zeros((2, half_part, RING * hidden_part), BF16)
    for k in range(RING):
        cut = pick(both_half, (zi + k) % RING, 1)
        cut = shift(cut, "fsdp", k) if k else cut
        both_cols = lax.dynamic_update_slice_in_dim(
            both_cols, cut, ((zi - k) % RING) * hidden_part, 2
        )
    down_sum, both_sum = lax.psum((down_half, both_cols), ("y", "x"))
    down_total = pair_gather(down_sum, dp, 0).reshape(hidden_part, width).astype(F32)
    both_total = pair_gather(both_sum, dp, 1).reshape(2, part, RING * hidden_part).astype(F32)

    grad_out_w = dot(attn_low, grad_branch, TN)
    grad_attn_low = dot(grad_branch, full_out, NT).astype(BF16)
    grad_query, grad_kv = attention_backward(
        first_row, query, kv_all, row_pos, grad_attn_low, attn_low, log_total
    )
    grad_kv = lax.all_to_all(grad_kv.reshape(RING * RING, tok, 2 * kv_width), ("y", "x"), 0, 0)
    grad_kv = jnp.sum(grad_kv.astype(F32), 0)
    grad_proj_query = rotate(grad_query, cosine, -sine_table).astype(BF16)
    grad_key_pre = rotate(grad_kv[:, :kv_width], cosine, -sine_table)
    grad_proj_kv = jnp.concatenate([grad_key_pre, grad_kv[:, kv_width:]], 1).astype(BF16)
    grad_bias = jnp.concatenate(
        [jnp.sum(g.astype(F32), 0) for g in (grad_proj_query, grad_proj_kv)]
    )
    grad_query_w = dot(normed_attn, grad_proj_query, TN)
    grad_kv_w = dot(normed_attn, grad_proj_kv, TN)
    grad_normed_attn = dot(grad_proj_query, w_query, NT) + dot(grad_proj_kv, w_kv, NT)
    grad_in_norm, grad_gain_attn = norm_back(grad_normed_attn, hidden_in, scale_attn, gain_attn)
    grad_input = (grad_mid + grad_in_norm).astype(BF16)

    early = jnp.concatenate([grad_out_w, grad_query_w], 1).astype(BF16)
    early = pair_scatter(early.reshape(RING, 2, half_part, -1), dp)
    early = ring_scatter(early, "fsdp", zi)
    sums = jnp.concatenate(
        [
            grad_gain_attn.reshape(RING, -1),
            grad_gain_mlp.reshape(RING, -1),
            grad_bias[:qk_width].reshape(RING, -1),
            grad_bias[qk_width:].reshape(RING, -1),
        ],
        1,
    )
    sums_width = sums.shape[1]
    sums = jnp.pad(sums, ((0, 0), (0, 2 * small_rows * 2 * kv_width - sums_width)))
    late = jnp.concatenate(
        [
            grad_kv_w.reshape(RING, 2, half_part, 2 * kv_width),
            sums.reshape(RING, 2, small_rows, 2 * kv_width),
        ],
        2,
    )
    late = pair_scatter(late, dp)
    late = ring_scatter(late, "fsdp", zi)
    joint = jnp.concatenate([jnp.pad(early, ((0, small_rows), (0, 0))), late], 1)
    joint = ring_scatter(joint.reshape(RING, -1, joint.shape[1]), "y", yi).astype(BF16)
    joint = jnp.sum(ring_gather(joint, "x", xi).astype(F32), 0).astype(BF16)
    joint = ring_gather(joint, "y", yi).reshape(half_part + small_rows, -1)
    joint = pair_gather(joint, dp, 0)
    weights = joint[:, :half_part].reshape(part, -1).astype(F32)
    sums = joint[:, half_part:, 2 * q_width :].reshape(-1)[:sums_width].astype(F32)
    qk_part = qk_width // RING
    return (
        layer_out[None],
        grad_input[None],
        sums[:part],
        weights[:, width:],
        sums[2 * part : 2 * part + qk_part],
        sums[2 * part + qk_part :],
        weights[:, :width],
        sums[part : 2 * part],
        both_total[0],
        both_total[1],
        down_total,
    )


def solution(mesh):
    devices = mesh.devices
    dp, ctx, fsdp = devices.shape
    fine = Mesh(devices.reshape(dp, RING, ctx // RING, fsdp), ("dp", "y", "x", "fsdp"))
    rows = P(("dp", "fsdp"), ("y", "x"), None)
    vec = P("fsdp")
    mat = P("fsdp", None)
    return jax.shard_map(
        per_device,
        mesh=fine,
        in_specs=(rows, vec, mat, vec, mat, vec, mat, mat, mat, rows),
        out_specs=(rows, rows, vec, mat, vec, vec, mat, vec, mat, mat, mat),
        check_vma=False,
    )
```

```python
import jax
import jax.numpy as jnp
from jax import lax
from jax.experimental import pallas as pl
from jax.experimental.pallas import tpu as pltpu
from jax.sharding import Mesh, PartitionSpec as P

HEADS = 14
KV = 2
HD = 64
GROUPS = HEADS // KV
RING = 4
KEY_BLOCK = 768

NORM_EPS = 1e-06
ROPE_THETA = 1000000.0
MASK_VALUE = -1e30

NT = (((1,), (1,)), ((), ()))
NN = (((1,), (0,)), ((), ()))
TN = (((0,), (0,)), ((), ()))
F32 = jnp.float32
BF16 = jnp.bfloat16


def dotf(a, b, dims):
    return lax.dot_general(a, b, dims, preferred_element_type=F32)


def key_parts(place_ref, kv_refs, step):
    def run(part, masked):
        def body(i, _):
            step(part, pl.multiple_of(i * KEY_BLOCK, KEY_BLOCK), masked)
            return 0

        lax.fori_loop(0, kv_refs[part].shape[0] // KEY_BLOCK, body, 0)

    run(0, True)
    for part in range(1, len(kv_refs)):
        pl.when(place_ref[0] >= part)(lambda part=part: run(part, False))


def mask_scores(s, row_ref, place_ref, start, tok):
    keys = start + lax.broadcasted_iota(jnp.int32, (s.shape[0], 1), 0)
    block = jnp.zeros(keys.shape, jnp.int32)
    for i in range(1, RING):
        block = block + (keys >= i * tok).astype(jnp.int32)
    keys = keys - 2 * tok * block
    keys = jnp.where(block <= place_ref[1], keys, 2 * RING * tok)
    return jnp.where(keys <= row_ref[0:1, :], s, MASK_VALUE)


def turn(values, cosine, sine):
    lane = lax.broadcasted_iota(jnp.int32, values.shape, 1)
    ahead = pltpu.roll(values, 2 * HD - HD // 2, 1)
    behind = pltpu.roll(values, HD // 2, 1)
    in_first = lax.rem(lane, HD) < HD // 2
    return values * cosine + jnp.where(in_first, ahead, behind) * sine


def stack_pair(values, pair, dst_ref, tok):
    for i in range(2):
        j, g = divmod(2 * pair + i, GROUPS)
        dst_ref[j, g * tok : (g + 1) * tok, :] = values[:, i * HD : (i + 1) * HD]


def unstack_pair(cols, pair, tok):
    two = []
    for h in (2 * pair, 2 * pair + 1):
        j, g = divmod(h, GROUPS)
        two.append(cols[j][:, g * tok : (g + 1) * tok])
    return jnp.concatenate(two, 0).T


def pair_lanes(pair):
    return slice(pair * 2 * HD, (pair + 1) * 2 * HD)


def fwd_kernel(
    place_ref, q_ref, cos_ref, sin_ref, row_ref, kv0, kv1, kv2, kv3,
    o_ref, lse_ref, qs, m_s, acc,
):
    tok = q_ref.shape[0]
    kv_refs = (kv0, kv1, kv2, kv3)
    for pair in range(HEADS // 2):
        turned = turn(q_ref[:, pair_lanes(pair)], cos_ref[...], sin_ref[...])
        stack_pair((turned.astype(BF16) * HD**-0.5).astype(BF16), pair, qs, tok)
    m_s[...] = jnp.full(m_s.shape, MASK_VALUE, F32)
    acc[...] = jnp.zeros(acc.shape, F32)

    def step(part, start, masked):
        kv = kv_refs[part][pl.ds(start, KEY_BLOCK), :]
        for j in range(KV):
            k = kv[:, j * HD : (j + 1) * HD]
            v = kv[:, (KV + j) * HD : (KV + j + 1) * HD]
            s = dotf(k, qs[j], NT)
            if masked:
                s = mask_scores(s, row_ref, place_ref, start, tok)
            m_old = m_s[j, 0:1, :]
            m_new = jnp.maximum(m_old, jnp.max(s, 0, keepdims=True))
            p = jnp.exp(s - m_new)
            vx = jnp.concatenate([v, jnp.ones((KEY_BLOCK, HD), BF16)], 1)
            acc[j] = acc[j] * jnp.exp(m_old - m_new) + dotf(vx, p.astype(BF16), TN)[: HD + 8]
            m_s[j, 0:1, :] = m_new

    key_parts(place_ref, kv_refs, step)
    cols = []
    for j in range(KV):
        total = acc[j, HD : HD + 1, :]
        cols.append(acc[j, :HD, :] / total)
        lse_ref[j, :, :] = jnp.broadcast_to(m_s[j, 0:1, :] + jnp.log(total), lse_ref.shape[1:])
    for pair in range(HEADS // 2):
        o_ref[:, pair_lanes(pair)] = unstack_pair(cols, pair, tok).astype(o_ref.dtype)


def bwd_kernel(
    place_ref, qs, cos_ref, sin_ref, row_ref, kv0, kv1, kv2, kv3, do_ref, o_ref, lse_ref,
    dq_ref, dkv0, dkv1, dkv2, dkv3, dos, delta_s, dq_s,
):
    tok = do_ref.shape[0]
    kv_refs = (kv0, kv1, kv2, kv3)
    dkv_refs = (dkv0, dkv1, dkv2, dkv3)
    for pair in range(HEADS // 2):
        stack_pair(do_ref[:, pair_lanes(pair)], pair, dos, tok)
    prod = do_ref[...].astype(F32) * o_ref[...].astype(F32)
    ones = jnp.ones((8, HD), F32)
    for h in range(HEADS):
        j, g = divmod(h, GROUPS)
        delta_s[j, :, g * tok : (g + 1) * tok] = lax.dot_general(
            ones,
            prod[:, h * HD : (h + 1) * HD],
            NT,
            precision=lax.Precision.HIGHEST,
            preferred_element_type=F32,
        )
    dq_s[...] = jnp.zeros(dq_s.shape, F32)

    def step(part, start, masked):
        kv = kv_refs[part][pl.ds(start, KEY_BLOCK), :]
        dk = []
        dv = []
        for j in range(KV):
            k = kv[:, j * HD : (j + 1) * HD]
            v = kv[:, (KV + j) * HD : (KV + j + 1) * HD]
            s = dotf(k, qs[j], NT)
            if masked:
                s = mask_scores(s, row_ref, place_ref, start, tok)
            p = jnp.exp(s - lse_ref[j, 0:1, :])
            dp = dotf(v, dos[j], NT)
            ds = (p * (dp - delta_s[j, 0:1, :])).astype(BF16)
            dv.append(dotf(p.astype(BF16), dos[j], NN))
            dk.append(dotf(ds, qs[j], NN))
            dq_s[j] += dotf(k, ds, TN)
        dkv_refs[part][pl.ds(start, KEY_BLOCK), :] = jnp.concatenate(dk + dv, 1).astype(BF16)

    key_parts(place_ref, kv_refs, step)
    for part in range(1, RING):

        def clear(part=part):
            dkv_refs[part][...] = jnp.zeros(dkv_refs[part].shape, BF16)

        pl.when(place_ref[0] < part)(clear)
    cols = [dq_s[j] * (HD**-0.5) for j in range(KV)]
    for pair in range(HEADS // 2):
        turned = turn(unstack_pair(cols, pair, tok), cos_ref[...], -sin_ref[...])
        dq_ref[:, pair_lanes(pair)] = turned.astype(dq_ref.dtype)


def kv_kernel(h_ref, w_ref, bias_ref, cos_ref, sin_ref, out_ref):
    keys = KV * HD
    proj = dotf(h_ref[...], w_ref[...], NN) + bias_ref[0:1, :]
    out_ref[:, :keys] = turn(proj[:, :keys], cos_ref[...], sin_ref[...]).astype(BF16)
    out_ref[:, keys:] = proj[:, keys:].astype(BF16)


def kv_back_kernel(p0, p1, p2, p3, cos_ref, sin_ref, out_ref):
    keys = KV * HD
    total = p0[...].astype(F32) + p1[...].astype(F32) + p2[...].astype(F32) + p3[...].astype(F32)
    out_ref[:, :keys] = turn(total[:, :keys], cos_ref[...], -sin_ref[...]).astype(BF16)
    out_ref[:, keys:] = total[:, keys:].astype(BF16)


VM = pl.BlockSpec(memory_space=pltpu.VMEM)
SM = pl.BlockSpec(memory_space=pltpu.SMEM)


def attention_cost(tok, keys, products):
    return pl.CostEstimate(
        flops=products * 2 * HEADS * tok * keys * HD * 4,
        bytes_accessed=4 * 2**20,
        transcendentals=HEADS * tok * keys,
    )


def project_kv(normed, weight, bias, tables):
    shape = (normed.shape[0], weight.shape[1])
    return pl.pallas_call(
        kv_kernel,
        out_shape=jax.ShapeDtypeStruct(shape, BF16),
        in_specs=[VM] * 5,
        out_specs=VM,
        cost_estimate=pl.CostEstimate(
            flops=2 * normed.size * shape[1], bytes_accessed=2**20, transcendentals=0
        ),
    )(normed, weight, jnp.broadcast_to(bias[None], (8, shape[1])), *tables)


def sum_kv(parts, tables):
    return pl.pallas_call(
        kv_back_kernel,
        out_shape=jax.ShapeDtypeStruct(parts[0].shape, BF16),
        in_specs=[VM] * (RING + 2),
        out_specs=VM,
        cost_estimate=pl.CostEstimate(flops=2**18, bytes_accessed=2**20, transcendentals=0),
    )(*parts, *tables)


def attention_forward(where, q, tables, row_index, kv_parts):
    tok = q.shape[0]
    rows = GROUPS * tok
    return pl.pallas_call(
        fwd_kernel,
        out_shape=(
            jax.ShapeDtypeStruct(q.shape, BF16),
            jax.ShapeDtypeStruct((KV, 8, rows), F32),
            jax.ShapeDtypeStruct((KV, rows, HD), BF16),
        ),
        in_specs=[SM] + [VM] * 8,
        out_specs=(VM, VM, VM),
        scratch_shapes=[
            pltpu.VMEM((KV, 8, rows), F32),
            pltpu.VMEM((KV, HD + 8, rows), F32),
        ],
        compiler_params=pltpu.CompilerParams(vmem_limit_bytes=48 * 2**20),
        cost_estimate=attention_cost(tok, RING * kv_parts[0].shape[0], 2),
    )(where, q, *tables, row_index, *kv_parts)


def attention_backward(where, q, tables, row_index, kv_parts, do, o, lse):
    tok = do.shape[0]
    rows = GROUPS * tok
    out = pl.pallas_call(
        bwd_kernel,
        out_shape=(
            jax.ShapeDtypeStruct(do.shape, BF16),
            *[jax.ShapeDtypeStruct(kv.shape, BF16) for kv in kv_parts],
        ),
        in_specs=[SM] + [VM] * 11,
        out_specs=(VM,) * 5,
        scratch_shapes=[
            pltpu.VMEM((KV, rows, HD), BF16),
            pltpu.VMEM((KV, 8, rows), F32),
            pltpu.VMEM((KV, HD, rows), F32),
        ],
        compiler_params=pltpu.CompilerParams(vmem_limit_bytes=48 * 2**20),
        cost_estimate=attention_cost(tok, RING * kv_parts[0].shape[0], 5),
    )(where, q, *tables, row_index, *kv_parts, do, o, lse)
    return out[0], out[1:]


def rope_tables(positions, head_size):
    half_size = head_size // 2
    frequency = ROPE_THETA ** (-jnp.arange(half_size, dtype=jnp.float32) * 2.0 / head_size)
    angles = positions.astype(jnp.float32)[:, None] * frequency[None, :]
    cosine, sine = jnp.cos(angles), jnp.sin(angles)
    return (
        jnp.concatenate([cosine] * 4, 1),
        jnp.concatenate([-sine, sine] * 2, 1),
    )


def inverse_rms(values):
    return lax.rsqrt(jnp.mean(values * values, -1, keepdims=True) + NORM_EPS)


def norm_back(grad_rows, values, row_scale, gain_row):
    grad_normed = grad_rows * gain_row
    cubed = row_scale * row_scale * row_scale
    grad_values = row_scale * grad_normed - values * cubed * jnp.mean(
        grad_normed * values, -1, keepdims=True
    )
    grad_gain = jnp.sum(grad_rows * values * row_scale, 0)
    return (grad_values, grad_gain)


def dot(left, right, dims=NN):
    return lax.dot_general(left, right, dims, preferred_element_type=F32)


def shift(values, axis, step):
    return lax.ppermute(values, axis, [(i, (i + step) % RING) for i in range(RING)])


def swap(values):
    return lax.ppermute(values, "dp", [(0, 1), (1, 0)])


def after(values, *others):
    return lax.optimization_barrier((values, others))[0]


def pick(values, index, axis=0):
    return lax.dynamic_index_in_dim(values, index, axis, keepdims=False)


def place_kernel(me_ref, p0, p1, p2, p3, out_ref):
    rows = p0.shape[0]
    for k, ref in enumerate((p0, p1, p2, p3)):
        slot = lax.rem(me_ref[0] + (RING - k), RING)
        out_ref[pl.ds(pl.multiple_of(slot * rows, rows), rows), :] = ref[...]


def place_rows(parts, me):
    rows, cols = parts[0].shape
    return pl.pallas_call(
        place_kernel,
        out_shape=jax.ShapeDtypeStruct((RING * rows, cols), parts[0].dtype),
        in_specs=[SM] + [VM] * RING,
        out_specs=VM,
        compiler_params=pltpu.CompilerParams(vmem_limit_bytes=32 * 2**20),
        cost_estimate=pl.CostEstimate(
            flops=0, bytes_accessed=4 * RING * rows * cols, transcendentals=0
        ),
    )(me, *parts)


def sums_kernel(step, here_ref, mine, other, first_ref, second_ref, down_ref):
    blocks, total, cols = mine.shape[1:]
    rows = first_ref.shape[0]
    down_rows, width = down_ref.shape[2:]
    down_step = total - RING * step

    def lay(source, out_ref, half):
        for x in range(blocks):
            size = min(step, rows - x * step)
            for a in range(RING):
                slot = lax.rem(here_ref[0] + (RING - a), RING)
                start = pl.multiple_of(slot * step, step)
                value = source[0, x, pl.ds(start, step), :][:size].astype(F32)
                out_ref[x * step : x * step + size, a * cols : (a + 1) * cols] = value
            size = min(down_step, down_rows - x * down_step)
            value = source[0, x, RING * step :, :width][:size].astype(F32)
            down_ref[half, 0, x * down_step : x * down_step + size, :] = value

    @pl.when(here_ref[1] == 0)
    def _():
        lay(mine, first_ref, 0)
        lay(other, second_ref, 1)

    @pl.when(here_ref[1] != 0)
    def _():
        lay(other, first_ref, 0)
        lay(mine, second_ref, 1)


def place_sums(mine, other, here, step, rows, down_rows, width):
    _, blocks, total, cols = mine.shape
    part = pl.BlockSpec((1, blocks, total, cols), lambda i: (i, 0, 0, 0))
    whole = pl.BlockSpec((rows, RING * cols), lambda i: (i, 0))
    halves = pl.BlockSpec((2, 1, down_rows, width), lambda i: (0, i, 0, 0))
    shape = jax.ShapeDtypeStruct((RING * rows, RING * cols), F32)
    return pl.pallas_call(
        lambda *refs: sums_kernel(step, *refs),
        grid=(RING,),
        out_shape=(shape, shape, jax.ShapeDtypeStruct((2, RING, down_rows, width), F32)),
        in_specs=[SM, part, part],
        out_specs=(whole, whole, halves),
        compiler_params=pltpu.CompilerParams(vmem_limit_bytes=48 * 2**20),
        cost_estimate=pl.CostEstimate(
            flops=0, bytes_accessed=12 * RING * RING * rows * cols, transcendentals=0
        ),
    )(here, mine, other)


def outer_kernel(a_ref, b_ref, *refs):
    product = dotf(a_ref[...], b_ref[...], TN)
    if len(refs) > 1:
        product = product + refs[0][...].astype(F32)
    refs[-1][...] = product.astype(BF16)


def outer(left, right, *more):
    shape = (left.shape[1], right.shape[1])
    return pl.pallas_call(
        outer_kernel,
        out_shape=jax.ShapeDtypeStruct(shape, BF16),
        in_specs=[VM] * (2 + len(more)),
        out_specs=VM,
        compiler_params=pltpu.CompilerParams(vmem_limit_bytes=40 * 2**20),
        cost_estimate=pl.CostEstimate(
            flops=2 * left.size * shape[1], bytes_accessed=2**20, transcendentals=0
        ),
    )(left, right, *more)


def ring_parts(values, axis):
    return [values] + [shift(values, axis, k) for k in (1, 2, 3)]


def ring_return(parts, axis):
    total = parts[0].astype(F32)
    for k in (1, 2, 3):
        total = total + shift(parts[k].astype(BF16), axis, -k).astype(F32)
    return total


def ring_scatter(parts, axis, me):
    total = pick(parts, me).astype(F32)
    for k in (1, 2, 3):
        total = total + shift(pick(parts, (me + k) % RING).astype(BF16), axis, k).astype(F32)
    return total


def per_device(tokens, norm_attn, w_qkv, b_qkv, w_out, norm_mlp, w_gate, w_up, w_down, cotangent):
    tok = tokens.shape[1]
    width = tokens.shape[2]
    part = norm_attn.shape[0]
    q_width = HEADS * HD
    kv_width = KV * HD
    qk_width = q_width + kv_width
    bias_part = b_qkv.shape[0]
    hidden_part = w_down.shape[0]
    second = lax.axis_index("dp") == 1
    yi = lax.axis_index("y")
    xi = lax.axis_index("x")
    zi = lax.axis_index("fsdp")
    where = jnp.stack([yi, xi]).astype(jnp.int32)
    here = jnp.stack([zi, lax.axis_index("dp")]).astype(jnp.int32)
    hidden_in = tokens[0].astype(F32)
    grad_out = cotangent[0]
    positions = (yi * RING + xi) * tok + jnp.arange(tok, dtype=jnp.int32)
    row_index = jnp.broadcast_to(
        jnp.tile(jnp.arange(tok, dtype=jnp.int32), GROUPS)[None], (8, GROUPS * tok)
    )
    tables = rope_tables(positions, HD)

    def choose(first, other):
        return jnp.where(second, other, first)

    small = jnp.concatenate([norm_attn, b_qkv, norm_mlp])
    small_rows = 16
    small = jnp.pad(small, (0, small_rows * 2 * kv_width - small.shape[0]))
    first_weights = lax.all_gather(
        jnp.concatenate([w_qkv[:, q_width:], small.reshape(small_rows, 2 * kv_width)], 0),
        "fsdp",
        axis=0,
    )
    w_kv = first_weights[:, :part].reshape(width, 2 * kv_width)
    vectors = first_weights[:, part:].reshape(RING, small_rows * 2 * kv_width)
    gain_attn = vectors[:, :part].reshape(-1).astype(F32)
    bias = vectors[:, part : part + bias_part].reshape(-1).astype(F32)
    gain_mlp = vectors[:, part + bias_part : 2 * part + bias_part].reshape(-1).astype(F32)

    square_mine = choose(w_qkv[:, :q_width], w_out)
    square_mine = lax.all_gather(square_mine, "fsdp", axis=0, tiled=True)

    scale_attn = inverse_rms(hidden_in)
    normed_attn = (hidden_in * scale_attn * gain_attn).astype(BF16)
    kv_local = project_kv(normed_attn, w_kv, bias[q_width:], tables)
    kv_row = jnp.concatenate(ring_parts(kv_local, "x"), 0)

    square_mine = after(square_mine, kv_row)
    square_other = swap(square_mine)
    kv_parts = ring_parts(kv_row, "y")
    w_query = choose(square_mine, square_other)
    full_out = choose(square_other, square_mine)
    query = dot(normed_attn, w_query) + bias[:q_width]

    wide = after(choose(w_gate, w_up), square_mine, kv_row)
    pieces = []
    for k in range(RING):
        cut = lax.dynamic_slice_in_dim(wide, ((zi + k) % RING) * hidden_part, hidden_part, 1)
        pieces.append(shift(cut, "fsdp", k) if k else cut)

    grad_out_parts = ring_parts(after(grad_out, wide), "fsdp")

    attn_low, log_total, query = attention_forward(where, query, tables, row_index, kv_parts)
    attn_low, grad_out_parts, pieces = lax.optimization_barrier(
        (attn_low, grad_out_parts, pieces)
    )
    hidden_mid = hidden_in + dot(attn_low, full_out)
    scale_mlp = inverse_rms(hidden_mid)
    normed_mlp = (hidden_mid * scale_mlp * gain_mlp).astype(BF16)
    normed_group = jnp.concatenate(ring_parts(normed_mlp, "fsdp"), 0)
    grad_out_group = jnp.concatenate(grad_out_parts, 0)
    wide_mine = place_rows(pieces, here)
    wide_other = swap(wide_mine.reshape(RING, part, hidden_part)).reshape(width, hidden_part)

    act_mine = dot(normed_group, wide_mine)
    act_other = dot(normed_group, wide_other)
    gate_act = choose(act_mine, act_other)
    up_act = choose(act_other, act_mine)
    sigmoid_gate = jax.nn.sigmoid(gate_act)
    silu_gate = gate_act * sigmoid_gate
    mixed = (silu_gate * up_act).astype(BF16)
    grad_mixed = dot(grad_out_group, w_down, NT)
    grad_gate = grad_mixed * up_act * sigmoid_gate * (1.0 + gate_act * (1.0 - sigmoid_gate))
    grad_up = grad_mixed * silu_gate
    grad_mine = choose(grad_gate, grad_up).astype(BF16)
    grad_other = choose(grad_up, grad_gate).astype(BF16)
    grad_normed_part = dot(grad_mine, wide_mine, NT) + dot(grad_other, wide_other, NT)
    grad_normed_part = grad_normed_part.reshape(RING, tok, width)
    returned = [grad_normed_part[0]] + [
        shift(grad_normed_part[k].astype(BF16), "fsdp", -k) for k in (1, 2, 3)
    ]

    half = hidden_part // 2
    down_low = outer(mixed, grad_out_group)
    wide_sent = swap(outer(normed_group, grad_other).reshape(RING, part, hidden_part))
    down_mine = choose(down_low[:half], down_low[half:])
    down_sent = swap(choose(down_low[half:], down_low[:half]))
    wide_sum = outer(normed_group, grad_mine, wide_sent.reshape(width, hidden_part))
    down_sum = (down_mine.astype(F32) + down_sent.astype(F32)).astype(BF16)
    quarter = part // RING
    wide_sum = wide_sum.reshape(RING, RING, quarter, hidden_part)
    wide_cut = [pick(wide_sum, (yi + k) % RING, 1) for k in range(RING)]
    down_sum = down_sum.reshape(RING, half // RING, width)
    down_cut = [pick(down_sum, (yi + k) % RING) for k in range(RING)]
    returned, wide_cut, down_cut = lax.optimization_barrier((returned, wide_cut, down_cut))
    wide_cut = [shift(v, "y", k) if k else v for k, v in enumerate(wide_cut)]
    down_cut = [shift(v, "y", k) if k else v for k, v in enumerate(down_cut)]

    grad_normed_mlp = sum(p.astype(F32) for p in returned)
    grad_mid_norm, grad_gain_mlp = norm_back(grad_normed_mlp, hidden_mid, scale_mlp, gain_mlp)
    grad_mid = grad_out.astype(F32) + grad_mid_norm
    grad_branch = grad_mid.astype(BF16)

    grad_attn_low = dot(grad_branch, full_out, NT).astype(BF16)
    grad_proj_query, grad_kv_parts = attention_backward(
        where, query, tables, row_index, kv_parts, grad_attn_low, attn_low, log_total
    )
    wide_y = sum(v.astype(F32) for v in wide_cut).astype(BF16)
    down_y = sum(v.astype(F32) for v in down_cut).astype(BF16)
    wide_y, down_y, grad_kv_parts = lax.optimization_barrier((wide_y, down_y, grad_kv_parts))

    grad_kv_row = ring_return(grad_kv_parts, "y").astype(BF16)
    square_sent = swap(
        dot(
            choose(attn_low, normed_attn), choose(grad_branch, grad_proj_query), TN
        ).astype(BF16)
    )
    square_sum = dot(choose(normed_attn, attn_low), choose(grad_proj_query, grad_branch), TN)
    square_sum = (square_sum + square_sent.astype(F32)).astype(BF16)
    square_sum = ring_scatter(square_sum.reshape(RING, part, width), "fsdp", zi)

    grad_kv_row = grad_kv_row.reshape(RING, tok, 2 * kv_width)
    grad_kv_own = [shift(grad_kv_row[k], "x", -k) if k else grad_kv_row[0] for k in range(RING)]
    square_sum = square_sum.astype(BF16)
    out_part = dot(after(mixed, square_sent), w_down).astype(BF16).reshape(RING, tok, width)
    grad_kv_own, square_sum, out_part = lax.optimization_barrier(
        (grad_kv_own, square_sum, out_part)
    )
    layer_out = (hidden_mid + ring_return(out_part, "fsdp")).astype(BF16)
    grad_proj_kv = sum_kv(grad_kv_own, tables)
    wide_y, down_y, grad_proj_kv = lax.optimization_barrier((wide_y, down_y, grad_proj_kv))
    wide_row = -(-quarter // (16 * RING)) * 16
    down_row = -(-half // (8 * RING * RING)) * 8
    wide_y = jnp.pad(wide_y, ((0, 0), (0, RING * wide_row - quarter), (0, 0)))
    wide_y = wide_y.reshape(RING, RING, wide_row, hidden_part)
    down_y = jnp.pad(down_y, ((0, RING * down_row - half // RING), (0, 0)))
    down_y = down_y.reshape(RING, down_row, width)
    wide_x = pick(wide_y, xi, 1).astype(F32)
    down_x = pick(down_y, xi).astype(F32)
    for k in (1, 2, 3):
        wide_x = wide_x + shift(pick(wide_y, (xi + k) % RING, 1), "x", k).astype(F32)
        down_x = down_x + shift(pick(down_y, (xi + k) % RING), "x", k).astype(F32)
    wide_x = wide_x.astype(BF16)
    cols = [pick(wide_x, (zi + k) % RING) for k in range(RING)]
    cols = [shift(v, "fsdp", k) if k else v for k, v in enumerate(cols)]
    down_x = jnp.pad(down_x.astype(BF16), ((0, 0), (0, hidden_part - width)))
    total = lax.all_gather(jnp.concatenate(cols + [down_x], 0), ("y", "x"), axis=0, tiled=True)

    bias_query = jnp.sum(grad_proj_query.astype(F32), 0)
    bias_kv = jnp.sum(grad_proj_kv.astype(F32), 0)
    grad_normed_attn = dot(grad_proj_query, w_query, NT) + dot(grad_proj_kv, w_kv, NT)
    grad_in_norm, grad_gain_attn = norm_back(grad_normed_attn, hidden_in, scale_attn, gain_attn)
    grad_input = (grad_mid + grad_in_norm).astype(BF16)

    extra = 32
    qk_part = qk_width // RING
    kv_part = kv_width // RING

    def narrow(weight, long, short):
        rows = jnp.concatenate([long.reshape(RING, -1), short.reshape(RING, -1)], 1)
        rows = jnp.pad(rows, ((0, 0), (0, extra * kv_width - rows.shape[1])))
        return jnp.concatenate(
            [weight.reshape(RING, part, kv_width), rows.reshape(RING, extra, kv_width)], 1
        )

    grad_kv_w = dot(normed_attn, grad_proj_kv, TN)
    late_first = narrow(
        grad_kv_w[:, :kv_width],
        grad_gain_attn,
        jnp.concatenate([bias_query, bias_kv[:kv_width]]),
    )
    late_second = narrow(grad_kv_w[:, kv_width:], grad_gain_mlp, bias_kv[kv_width:])
    late = choose(late_first, late_second)
    late = late + swap(choose(late_second, late_first).astype(BF16)).astype(F32)
    late = ring_scatter(late, "fsdp", zi)
    joint = jnp.concatenate([jnp.pad(square_sum, ((0, extra), (0, 0))), late.astype(BF16)], 1)
    joint = ring_scatter(joint.reshape(RING, -1, joint.shape[1]), "y", yi).astype(BF16)
    joint, layer_out = lax.optimization_barrier((joint, layer_out))
    shares = ring_parts(joint, "x")
    joint = sum(
        pick(jnp.stack(shares), (xi - i) % RING).astype(F32) for i in range(RING)
    ).astype(BF16)
    joint = place_rows(ring_parts(joint, "y"), where)
    joint_other = swap(joint)
    joint_first = choose(joint, joint_other).astype(F32)
    joint_second = choose(joint_other, joint).astype(F32)
    grad_qkv_w = jnp.concatenate([joint_first[:part], joint_second[:part, width:]], 1)
    grad_out_w = joint_second[:part, :width]
    sums_first = joint_first[part:, width:].reshape(-1)
    sums_second = joint_second[part:, width:].reshape(-1)

    total = total.reshape(RING, RING, RING * wide_row + down_row, hidden_part)
    grad_gate_w, grad_up_w, grad_down_w = place_sums(
        total, swap(total), here, wide_row, quarter, half // RING, width
    )
    grad_down_w = grad_down_w.reshape(hidden_part, width)
    return (
        layer_out[None],
        grad_input[None],
        sums_first[:part],
        grad_qkv_w,
        sums_first[part : part + qk_part],
        sums_second[part : part + kv_part],
        grad_out_w,
        sums_second[:part],
        grad_gate_w,
        grad_up_w,
        grad_down_w,
    )


def solution(mesh):
    devices = mesh.devices
    dp, ctx, fsdp = devices.shape
    fine = Mesh(devices.reshape(dp, RING, ctx // RING, fsdp), ("dp", "y", "x", "fsdp"))
    rows = P(("dp", "fsdp"), ("y", "x"), None)
    vec = P("fsdp")
    mat = P("fsdp", None)
    return jax.shard_map(
        per_device,
        mesh=fine,
        in_specs=(rows, vec, mat, vec, mat, vec, mat, mat, mat, rows),
        out_specs=(rows, rows, vec, mat, vec, vec, mat, vec, mat, mat, mat),
        check_vma=False,
    )
```

```python
import jax
import jax.numpy as jnp
from jax import lax
from jax.experimental import pallas as pl
from jax.experimental.pallas import tpu as pltpu
from jax.sharding import Mesh, PartitionSpec as P

HEADS = 14
KV = 2
HD = 64
GROUPS = HEADS // KV
RING = 4
KEY_BLOCK = 768

NORM_EPS = 1e-06
ROPE_THETA = 1000000.0
MASK_VALUE = -1e30

NT = (((1,), (1,)), ((), ()))
NN = (((1,), (0,)), ((), ()))
TN = (((0,), (0,)), ((), ()))
F32 = jnp.float32
BF16 = jnp.bfloat16


def dotf(a, b, dims):
    return lax.dot_general(a, b, dims, preferred_element_type=F32)


def key_parts(place_ref, kv_refs, step):
    def run(part, masked):
        def body(i, _):
            step(part, pl.multiple_of(i * KEY_BLOCK, KEY_BLOCK), masked)
            return 0

        lax.fori_loop(0, kv_refs[part].shape[0] // KEY_BLOCK, body, 0)

    run(0, True)
    for part in range(1, len(kv_refs)):
        pl.when(place_ref[0] >= part)(lambda part=part: run(part, False))


def mask_scores(s, row_ref, place_ref, start, tok):
    keys = start + lax.broadcasted_iota(jnp.int32, (s.shape[0], 1), 0)
    block = jnp.zeros(keys.shape, jnp.int32)
    for i in range(1, RING):
        block = block + (keys >= i * tok).astype(jnp.int32)
    keys = keys - 2 * tok * block
    keys = jnp.where(block <= place_ref[1], keys, 2 * RING * tok)
    return jnp.where(keys <= row_ref[0:1, :], s, MASK_VALUE)


def turn(values, cosine, sine):
    lane = lax.broadcasted_iota(jnp.int32, values.shape, 1)
    ahead = pltpu.roll(values, 2 * HD - HD // 2, 1)
    behind = pltpu.roll(values, HD // 2, 1)
    in_first = lax.rem(lane, HD) < HD // 2
    return values * cosine + jnp.where(in_first, ahead, behind) * sine


def stack_pair(values, pair, dst_ref, tok):
    for i in range(2):
        j, g = divmod(2 * pair + i, GROUPS)
        dst_ref[j, g * tok : (g + 1) * tok, :] = values[:, i * HD : (i + 1) * HD]


def unstack_pair(cols, pair, tok):
    two = []
    for h in (2 * pair, 2 * pair + 1):
        j, g = divmod(h, GROUPS)
        two.append(cols[j][:, g * tok : (g + 1) * tok])
    return jnp.concatenate(two, 0).T


def pair_lanes(pair):
    return slice(pair * 2 * HD, (pair + 1) * 2 * HD)


def fwd_kernel(
    place_ref, q_ref, cos_ref, sin_ref, row_ref, kv0, kv1, kv2, kv3,
    o_ref, lse_ref, qs, m_s, acc,
):
    tok = q_ref.shape[0]
    kv_refs = (kv0, kv1, kv2, kv3)
    for pair in range(HEADS // 2):
        turned = turn(q_ref[:, pair_lanes(pair)], cos_ref[...], sin_ref[...])
        stack_pair((turned.astype(BF16) * HD**-0.5).astype(BF16), pair, qs, tok)
    m_s[...] = jnp.full(m_s.shape, MASK_VALUE, F32)
    acc[...] = jnp.zeros(acc.shape, F32)

    def step(part, start, masked):
        kv = kv_refs[part][pl.ds(start, KEY_BLOCK), :]
        for j in range(KV):
            k = kv[:, j * HD : (j + 1) * HD]
            v = kv[:, (KV + j) * HD : (KV + j + 1) * HD]
            s = dotf(k, qs[j], NT)
            if masked:
                s = mask_scores(s, row_ref, place_ref, start, tok)
            m_old = m_s[j, 0:1, :]
            m_new = jnp.maximum(m_old, jnp.max(s, 0, keepdims=True))
            p = jnp.exp(s - m_new)
            vx = jnp.concatenate([v, jnp.ones((KEY_BLOCK, HD), BF16)], 1)
            acc[j] = acc[j] * jnp.exp(m_old - m_new) + dotf(vx, p.astype(BF16), TN)[: HD + 8]
            m_s[j, 0:1, :] = m_new

    key_parts(place_ref, kv_refs, step)
    cols = []
    for j in range(KV):
        total = acc[j, HD : HD + 1, :]
        cols.append(acc[j, :HD, :] / total)
        lse_ref[j, :, :] = jnp.broadcast_to(m_s[j, 0:1, :] + jnp.log(total), lse_ref.shape[1:])
    for pair in range(HEADS // 2):
        o_ref[:, pair_lanes(pair)] = unstack_pair(cols, pair, tok).astype(o_ref.dtype)


def bwd_kernel(
    place_ref, qs, cos_ref, sin_ref, row_ref, kv0, kv1, kv2, kv3, do_ref, o_ref, lse_ref,
    dq_ref, dkv0, dkv1, dkv2, dkv3, dos, delta_s, dq_s,
):
    tok = do_ref.shape[0]
    kv_refs = (kv0, kv1, kv2, kv3)
    dkv_refs = (dkv0, dkv1, dkv2, dkv3)
    for pair in range(HEADS // 2):
        stack_pair(do_ref[:, pair_lanes(pair)], pair, dos, tok)
    prod = do_ref[...].astype(F32) * o_ref[...].astype(F32)
    ones = jnp.ones((8, HD), F32)
    for h in range(HEADS):
        j, g = divmod(h, GROUPS)
        delta_s[j, :, g * tok : (g + 1) * tok] = lax.dot_general(
            ones,
            prod[:, h * HD : (h + 1) * HD],
            NT,
            precision=lax.Precision.HIGHEST,
            preferred_element_type=F32,
        )
    dq_s[...] = jnp.zeros(dq_s.shape, F32)

    def step(part, start, masked):
        kv = kv_refs[part][pl.ds(start, KEY_BLOCK), :]
        dk = []
        dv = []
        for j in range(KV):
            k = kv[:, j * HD : (j + 1) * HD]
            v = kv[:, (KV + j) * HD : (KV + j + 1) * HD]
            s = dotf(k, qs[j], NT)
            if masked:
                s = mask_scores(s, row_ref, place_ref, start, tok)
            p = jnp.exp(s - lse_ref[j, 0:1, :])
            dp = dotf(v, dos[j], NT)
            ds = (p * (dp - delta_s[j, 0:1, :])).astype(BF16)
            dv.append(dotf(p.astype(BF16), dos[j], NN))
            dk.append(dotf(ds, qs[j], NN))
            dq_s[j] += dotf(k, ds, TN)
        dkv_refs[part][pl.ds(start, KEY_BLOCK), :] = jnp.concatenate(dk + dv, 1).astype(BF16)

    key_parts(place_ref, kv_refs, step)
    for part in range(1, RING):

        def clear(part=part):
            dkv_refs[part][...] = jnp.zeros(dkv_refs[part].shape, BF16)

        pl.when(place_ref[0] < part)(clear)
    cols = [dq_s[j] * (HD**-0.5) for j in range(KV)]
    for pair in range(HEADS // 2):
        turned = turn(unstack_pair(cols, pair, tok), cos_ref[...], -sin_ref[...])
        dq_ref[:, pair_lanes(pair)] = turned.astype(dq_ref.dtype)


def kv_kernel(h_ref, w_ref, bias_ref, cos_ref, sin_ref, out_ref):
    keys = KV * HD
    proj = dotf(h_ref[...], w_ref[...], NN) + bias_ref[0:1, :]
    out_ref[:, :keys] = turn(proj[:, :keys], cos_ref[...], sin_ref[...]).astype(BF16)
    out_ref[:, keys:] = proj[:, keys:].astype(BF16)


def kv_back_kernel(p0, p1, p2, p3, cos_ref, sin_ref, out_ref):
    keys = KV * HD
    total = p0[...].astype(F32) + p1[...].astype(F32) + p2[...].astype(F32) + p3[...].astype(F32)
    out_ref[:, :keys] = turn(total[:, :keys], cos_ref[...], -sin_ref[...]).astype(BF16)
    out_ref[:, keys:] = total[:, keys:].astype(BF16)


VM = pl.BlockSpec(memory_space=pltpu.VMEM)
SM = pl.BlockSpec(memory_space=pltpu.SMEM)


def attention_cost(tok, keys, products):
    return pl.CostEstimate(
        flops=products * 2 * HEADS * tok * keys * HD * 4,
        bytes_accessed=4 * 2**20,
        transcendentals=HEADS * tok * keys,
    )


def project_kv(normed, weight, bias, tables):
    shape = (normed.shape[0], weight.shape[1])
    return pl.pallas_call(
        kv_kernel,
        out_shape=jax.ShapeDtypeStruct(shape, BF16),
        in_specs=[VM] * 5,
        out_specs=VM,
        cost_estimate=pl.CostEstimate(
            flops=2 * normed.size * shape[1], bytes_accessed=2**20, transcendentals=0
        ),
    )(normed, weight, jnp.broadcast_to(bias[None], (8, shape[1])), *tables)


def sum_kv(parts, tables):
    return pl.pallas_call(
        kv_back_kernel,
        out_shape=jax.ShapeDtypeStruct(parts[0].shape, BF16),
        in_specs=[VM] * (RING + 2),
        out_specs=VM,
        cost_estimate=pl.CostEstimate(flops=2**18, bytes_accessed=2**20, transcendentals=0),
    )(*parts, *tables)


def attention_forward(where, q, tables, row_index, kv_parts):
    tok = q.shape[0]
    rows = GROUPS * tok
    return pl.pallas_call(
        fwd_kernel,
        out_shape=(
            jax.ShapeDtypeStruct(q.shape, BF16),
            jax.ShapeDtypeStruct((KV, 8, rows), F32),
            jax.ShapeDtypeStruct((KV, rows, HD), BF16),
        ),
        in_specs=[SM] + [VM] * 8,
        out_specs=(VM, VM, VM),
        scratch_shapes=[
            pltpu.VMEM((KV, 8, rows), F32),
            pltpu.VMEM((KV, HD + 8, rows), F32),
        ],
        compiler_params=pltpu.CompilerParams(vmem_limit_bytes=48 * 2**20),
        cost_estimate=attention_cost(tok, RING * kv_parts[0].shape[0], 2),
    )(where, q, *tables, row_index, *kv_parts)


def attention_backward(where, q, tables, row_index, kv_parts, do, o, lse):
    tok = do.shape[0]
    rows = GROUPS * tok
    out = pl.pallas_call(
        bwd_kernel,
        out_shape=(
            jax.ShapeDtypeStruct(do.shape, BF16),
            *[jax.ShapeDtypeStruct(kv.shape, BF16) for kv in kv_parts],
        ),
        in_specs=[SM] + [VM] * 11,
        out_specs=(VM,) * 5,
        scratch_shapes=[
            pltpu.VMEM((KV, rows, HD), BF16),
            pltpu.VMEM((KV, 8, rows), F32),
            pltpu.VMEM((KV, HD, rows), F32),
        ],
        compiler_params=pltpu.CompilerParams(vmem_limit_bytes=48 * 2**20),
        cost_estimate=attention_cost(tok, RING * kv_parts[0].shape[0], 5),
    )(where, q, *tables, row_index, *kv_parts, do, o, lse)
    return out[0], out[1:]


def rope_tables(positions, head_size):
    half_size = head_size // 2
    frequency = ROPE_THETA ** (-jnp.arange(half_size, dtype=jnp.float32) * 2.0 / head_size)
    angles = positions.astype(jnp.float32)[:, None] * frequency[None, :]
    cosine, sine = jnp.cos(angles), jnp.sin(angles)
    return (
        jnp.concatenate([cosine] * 4, 1),
        jnp.concatenate([-sine, sine] * 2, 1),
    )


def inverse_rms(values):
    return lax.rsqrt(jnp.mean(values * values, -1, keepdims=True) + NORM_EPS)


def norm_back(grad_rows, values, row_scale, gain_row):
    grad_normed = grad_rows * gain_row
    cubed = row_scale * row_scale * row_scale
    grad_values = row_scale * grad_normed - values * cubed * jnp.mean(
        grad_normed * values, -1, keepdims=True
    )
    grad_gain = jnp.sum(grad_rows * values * row_scale, 0)
    return (grad_values, grad_gain)


def dot(left, right, dims=NN):
    return lax.dot_general(left, right, dims, preferred_element_type=F32)


def shift(values, axis, step):
    return lax.ppermute(values, axis, [(i, (i + step) % RING) for i in range(RING)])


def swap(values):
    return lax.ppermute(values, "dp", [(0, 1), (1, 0)])


def after(values, *others):
    return lax.optimization_barrier((values, others))[0]


def pick(values, index, axis=0):
    return lax.dynamic_index_in_dim(values, index, axis, keepdims=False)


def place_kernel(me_ref, p0, p1, p2, p3, out_ref):
    rows = p0.shape[0]
    for k, ref in enumerate((p0, p1, p2, p3)):
        slot = lax.rem(me_ref[0] + (RING - k), RING)
        out_ref[pl.ds(pl.multiple_of(slot * rows, rows), rows), :] = ref[...]


def place_rows(parts, me):
    rows, cols = parts[0].shape
    return pl.pallas_call(
        place_kernel,
        out_shape=jax.ShapeDtypeStruct((RING * rows, cols), parts[0].dtype),
        in_specs=[SM] + [VM] * RING,
        out_specs=VM,
        compiler_params=pltpu.CompilerParams(vmem_limit_bytes=32 * 2**20),
        cost_estimate=pl.CostEstimate(
            flops=0, bytes_accessed=4 * RING * rows * cols, transcendentals=0
        ),
    )(me, *parts)


def sums_kernel(step, here_ref, mine, other, first_ref, second_ref, down_ref):
    blocks, total, cols = mine.shape[1:]
    rows = first_ref.shape[0]
    down_rows, width = down_ref.shape[2:]
    down_step = total - RING * step

    def lay(source, out_ref, half):
        for x in range(blocks):
            size = min(step, rows - x * step)
            for a in range(RING):
                slot = lax.rem(here_ref[0] + (RING - a), RING)
                start = pl.multiple_of(slot * step, step)
                value = source[0, x, pl.ds(start, step), :][:size].astype(F32)
                out_ref[x * step : x * step + size, a * cols : (a + 1) * cols] = value
            size = min(down_step, down_rows - x * down_step)
            value = source[0, x, RING * step :, :width][:size].astype(F32)
            down_ref[half, 0, x * down_step : x * down_step + size, :] = value

    @pl.when(here_ref[1] == 0)
    def _():
        lay(mine, first_ref, 0)
        lay(other, second_ref, 1)

    @pl.when(here_ref[1] != 0)
    def _():
        lay(other, first_ref, 0)
        lay(mine, second_ref, 1)


def place_sums(mine, other, here, step, rows, down_rows, width):
    _, blocks, total, cols = mine.shape
    part = pl.BlockSpec((1, blocks, total, cols), lambda i: (i, 0, 0, 0))
    whole = pl.BlockSpec((rows, RING * cols), lambda i: (i, 0))
    halves = pl.BlockSpec((2, 1, down_rows, width), lambda i: (0, i, 0, 0))
    shape = jax.ShapeDtypeStruct((RING * rows, RING * cols), F32)
    return pl.pallas_call(
        lambda *refs: sums_kernel(step, *refs),
        grid=(RING,),
        out_shape=(shape, shape, jax.ShapeDtypeStruct((2, RING, down_rows, width), F32)),
        in_specs=[SM, part, part],
        out_specs=(whole, whole, halves),
        compiler_params=pltpu.CompilerParams(vmem_limit_bytes=48 * 2**20),
        cost_estimate=pl.CostEstimate(
            flops=0, bytes_accessed=12 * RING * RING * rows * cols, transcendentals=0
        ),
    )(here, mine, other)


def outer_kernel(a_ref, b_ref, *refs):
    product = dotf(a_ref[...], b_ref[...], TN)
    if len(refs) > 1:
        product = product + refs[0][...].astype(F32)
    refs[-1][...] = product.astype(BF16)


def outer(left, right, *more):
    shape = (left.shape[1], right.shape[1])
    return pl.pallas_call(
        outer_kernel,
        out_shape=jax.ShapeDtypeStruct(shape, BF16),
        in_specs=[VM] * (2 + len(more)),
        out_specs=VM,
        compiler_params=pltpu.CompilerParams(vmem_limit_bytes=40 * 2**20),
        cost_estimate=pl.CostEstimate(
            flops=2 * left.size * shape[1], bytes_accessed=2**20, transcendentals=0
        ),
    )(left, right, *more)


def ring_parts(values, axis):
    return [values] + [shift(values, axis, k) for k in (1, 2, 3)]


def ring_return(parts, axis):
    total = parts[0].astype(F32)
    for k in (1, 2, 3):
        total = total + shift(parts[k].astype(BF16), axis, -k).astype(F32)
    return total


def ring_scatter(parts, axis, me):
    total = pick(parts, me).astype(F32)
    for k in (1, 2, 3):
        total = total + shift(pick(parts, (me + k) % RING).astype(BF16), axis, k).astype(F32)
    return total


def per_device(tokens, norm_attn, w_qkv, b_qkv, w_out, norm_mlp, w_gate, w_up, w_down, cotangent):
    tok = tokens.shape[1]
    width = tokens.shape[2]
    part = norm_attn.shape[0]
    q_width = HEADS * HD
    kv_width = KV * HD
    qk_width = q_width + kv_width
    bias_part = b_qkv.shape[0]
    hidden_part = w_down.shape[0]
    second = lax.axis_index("dp") == 1
    yi = lax.axis_index("y")
    xi = lax.axis_index("x")
    zi = lax.axis_index("fsdp")
    where = jnp.stack([yi, xi]).astype(jnp.int32)
    here = jnp.stack([zi, lax.axis_index("dp")]).astype(jnp.int32)
    hidden_in = tokens[0].astype(F32)
    grad_out = cotangent[0]
    positions = (yi * RING + xi) * tok + jnp.arange(tok, dtype=jnp.int32)
    row_index = jnp.broadcast_to(
        jnp.tile(jnp.arange(tok, dtype=jnp.int32), GROUPS)[None], (8, GROUPS * tok)
    )
    tables = rope_tables(positions, HD)

    def choose(first, other):
        return jnp.where(second, other, first)

    small = jnp.concatenate([norm_attn, b_qkv, norm_mlp])
    small_rows = 16
    small = jnp.pad(small, (0, small_rows * 2 * kv_width - small.shape[0]))
    first_weights = lax.all_gather(
        jnp.concatenate([w_qkv[:, q_width:], small.reshape(small_rows, 2 * kv_width)], 0),
        "fsdp",
        axis=0,
    )
    w_kv = first_weights[:, :part].reshape(width, 2 * kv_width)
    vectors = first_weights[:, part:].reshape(RING, small_rows * 2 * kv_width)
    gain_attn = vectors[:, :part].reshape(-1).astype(F32)
    bias = vectors[:, part : part + bias_part].reshape(-1).astype(F32)
    gain_mlp = vectors[:, part + bias_part : 2 * part + bias_part].reshape(-1).astype(F32)

    square_mine = choose(w_qkv[:, :q_width], w_out)
    square_mine = lax.all_gather(square_mine, "fsdp", axis=0, tiled=True)

    scale_attn = inverse_rms(hidden_in)
    normed_attn = (hidden_in * scale_attn * gain_attn).astype(BF16)
    kv_local = project_kv(normed_attn, w_kv, bias[q_width:], tables)
    kv_row = jnp.concatenate(ring_parts(kv_local, "x"), 0)

    square_mine = after(square_mine, kv_row)
    square_other = swap(square_mine)
    kv_parts = ring_parts(kv_row, "y")
    w_query = choose(square_mine, square_other)
    full_out = choose(square_other, square_mine)
    query = dot(normed_attn, w_query) + bias[:q_width]

    wide = after(choose(w_gate, w_up), square_mine, kv_row)
    pieces = []
    for k in range(RING):
        cut = lax.dynamic_slice_in_dim(wide, ((zi + k) % RING) * hidden_part, hidden_part, 1)
        pieces.append(shift(cut, "fsdp", k) if k else cut)

    grad_out_parts = ring_parts(after(grad_out, wide), "fsdp")

    attn_low, log_total, query = attention_forward(where, query, tables, row_index, kv_parts)
    attn_low, grad_out_parts, pieces = lax.optimization_barrier(
        (attn_low, grad_out_parts, pieces)
    )
    hidden_mid = hidden_in + dot(attn_low, full_out)
    scale_mlp = inverse_rms(hidden_mid)
    normed_mlp = (hidden_mid * scale_mlp * gain_mlp).astype(BF16)
    normed_group = jnp.concatenate(ring_parts(normed_mlp, "fsdp"), 0)
    grad_out_group = jnp.concatenate(grad_out_parts, 0)
    wide_mine = place_rows(pieces, here)
    wide_other = swap(wide_mine.reshape(RING, part, hidden_part)).reshape(width, hidden_part)

    act_mine = dot(normed_group, wide_mine)
    act_other = dot(normed_group, wide_other)
    gate_act = choose(act_mine, act_other)
    up_act = choose(act_other, act_mine)
    sigmoid_gate = jax.nn.sigmoid(gate_act)
    silu_gate = gate_act * sigmoid_gate
    mixed = (silu_gate * up_act).astype(BF16)
    grad_mixed = dot(grad_out_group, w_down, NT)
    grad_gate = grad_mixed * up_act * sigmoid_gate * (1.0 + gate_act * (1.0 - sigmoid_gate))
    grad_up = grad_mixed * silu_gate
    grad_mine = choose(grad_gate, grad_up).astype(BF16)
    grad_other = choose(grad_up, grad_gate).astype(BF16)
    grad_normed_part = dot(grad_mine, wide_mine, NT) + dot(grad_other, wide_other, NT)
    grad_normed_part = grad_normed_part.reshape(RING, tok, width)
    returned = [grad_normed_part[0]] + [
        shift(grad_normed_part[k].astype(BF16), "fsdp", -k) for k in (1, 2, 3)
    ]

    half = hidden_part // 2
    down_low = outer(mixed, grad_out_group)
    wide_sent = swap(outer(normed_group, grad_other).reshape(RING, part, hidden_part))
    down_mine = choose(down_low[:half], down_low[half:])
    down_sent = swap(choose(down_low[half:], down_low[:half]))
    wide_sum = outer(normed_group, grad_mine, wide_sent.reshape(width, hidden_part))
    down_sum = (down_mine.astype(F32) + down_sent.astype(F32)).astype(BF16)
    quarter = part // RING
    wide_sum = wide_sum.reshape(RING, RING, quarter, hidden_part)
    wide_cut = [pick(wide_sum, (yi + k) % RING, 1) for k in range(RING)]
    down_sum = down_sum.reshape(RING, half // RING, width)
    down_cut = [pick(down_sum, (yi + k) % RING) for k in range(RING)]
    out_part = dot(mixed, w_down).astype(BF16).reshape(RING, tok, width)
    returned, wide_cut, down_cut, out_part = lax.optimization_barrier(
        (returned, wide_cut, down_cut, out_part)
    )
    wide_cut = [shift(v, "y", k) if k else v for k, v in enumerate(wide_cut)]
    down_cut = [shift(v, "y", k) if k else v for k, v in enumerate(down_cut)]

    grad_normed_mlp = sum(p.astype(F32) for p in returned)
    grad_mid_norm, grad_gain_mlp = norm_back(grad_normed_mlp, hidden_mid, scale_mlp, gain_mlp)
    grad_mid = grad_out.astype(F32) + grad_mid_norm
    grad_branch = grad_mid.astype(BF16)

    grad_attn_low = dot(grad_branch, full_out, NT).astype(BF16)
    grad_proj_query, grad_kv_parts = attention_backward(
        where, query, tables, row_index, kv_parts, grad_attn_low, attn_low, log_total
    )
    wide_y = sum(v.astype(F32) for v in wide_cut).astype(BF16)
    down_y = sum(v.astype(F32) for v in down_cut).astype(BF16)
    wide_y, down_y, grad_kv_parts = lax.optimization_barrier((wide_y, down_y, grad_kv_parts))

    grad_kv_row = ring_return(grad_kv_parts, "y").astype(BF16)
    wide_y, down_y, grad_kv_row = lax.optimization_barrier((wide_y, down_y, grad_kv_row))
    wide_row = -(-quarter // (16 * RING)) * 16
    down_row = -(-half // (8 * RING * RING)) * 8
    wide_y = jnp.pad(wide_y, ((0, 0), (0, RING * wide_row - quarter), (0, 0)))
    wide_y = wide_y.reshape(RING, RING, wide_row, hidden_part)
    down_y = jnp.pad(down_y, ((0, RING * down_row - half // RING), (0, 0)))
    down_y = down_y.reshape(RING, down_row, width)
    wide_x = pick(wide_y, xi, 1).astype(F32)
    down_x = pick(down_y, xi).astype(F32)
    for k in (1, 2, 3):
        wide_x = wide_x + shift(pick(wide_y, (xi + k) % RING, 1), "x", k).astype(F32)
        down_x = down_x + shift(pick(down_y, (xi + k) % RING), "x", k).astype(F32)
    wide_x = wide_x.astype(BF16)
    cols = [pick(wide_x, (zi + k) % RING) for k in range(RING)]
    cols = [shift(v, "fsdp", k) if k else v for k, v in enumerate(cols)]
    down_x = jnp.pad(down_x.astype(BF16), ((0, 0), (0, hidden_part - width)))
    total = lax.all_gather(jnp.concatenate(cols + [down_x], 0), ("y", "x"), axis=0, tiled=True)

    square_sent = swap(
        dot(
            choose(attn_low, normed_attn), choose(grad_branch, grad_proj_query), TN
        ).astype(BF16)
    )
    square_sum = dot(choose(normed_attn, attn_low), choose(grad_proj_query, grad_branch), TN)
    square_sum = (square_sum + square_sent.astype(F32)).astype(BF16)
    square_sum = ring_scatter(square_sum.reshape(RING, part, width), "fsdp", zi)

    grad_kv_row = grad_kv_row.reshape(RING, tok, 2 * kv_width)
    grad_kv_own = [shift(grad_kv_row[k], "x", -k) if k else grad_kv_row[0] for k in range(RING)]
    square_sum = square_sum.astype(BF16)
    grad_kv_own, square_sum = lax.optimization_barrier((grad_kv_own, square_sum))
    grad_proj_kv = sum_kv(grad_kv_own, tables)
    out_part = after(out_part, grad_proj_kv)
    layer_out = (hidden_mid + ring_return(out_part, "fsdp")).astype(BF16)
    bias_query = jnp.sum(grad_proj_query.astype(F32), 0)
    bias_kv = jnp.sum(grad_proj_kv.astype(F32), 0)
    grad_normed_attn = dot(grad_proj_query, w_query, NT) + dot(grad_proj_kv, w_kv, NT)
    grad_in_norm, grad_gain_attn = norm_back(grad_normed_attn, hidden_in, scale_attn, gain_attn)
    grad_input = (grad_mid + grad_in_norm).astype(BF16)

    extra = 32
    qk_part = qk_width // RING
    kv_part = kv_width // RING

    def narrow(weight, long, short):
        rows = jnp.concatenate([long.reshape(RING, -1), short.reshape(RING, -1)], 1)
        rows = jnp.pad(rows, ((0, 0), (0, extra * kv_width - rows.shape[1])))
        return jnp.concatenate(
            [weight.reshape(RING, part, kv_width), rows.reshape(RING, extra, kv_width)], 1
        )

    grad_kv_w = dot(normed_attn, grad_proj_kv, TN)
    late_first = narrow(
        grad_kv_w[:, :kv_width],
        grad_gain_attn,
        jnp.concatenate([bias_query, bias_kv[:kv_width]]),
    )
    late_second = narrow(grad_kv_w[:, kv_width:], grad_gain_mlp, bias_kv[kv_width:])
    late = choose(late_first, late_second)
    late = late + swap(choose(late_second, late_first).astype(BF16)).astype(F32)
    late = ring_scatter(late, "fsdp", zi)
    joint = jnp.concatenate([jnp.pad(square_sum, ((0, extra), (0, 0))), late.astype(BF16)], 1)
    joint = ring_scatter(joint.reshape(RING, -1, joint.shape[1]), "y", yi).astype(BF16)
    shares = ring_parts(joint, "x")
    joint = sum(
        pick(jnp.stack(shares), (xi - i) % RING).astype(F32) for i in range(RING)
    ).astype(BF16)
    joint = place_rows(ring_parts(joint, "y"), where)
    joint, total = lax.optimization_barrier((joint, total))
    joint_other = swap(joint)
    joint_first = choose(joint, joint_other).astype(F32)
    joint_second = choose(joint_other, joint).astype(F32)
    grad_qkv_w = jnp.concatenate([joint_first[:part], joint_second[:part, width:]], 1)
    grad_out_w = joint_second[:part, :width]
    sums_first = joint_first[part:, width:].reshape(-1)
    sums_second = joint_second[part:, width:].reshape(-1)

    total = total.reshape(RING, RING, RING * wide_row + down_row, hidden_part)
    grad_gate_w, grad_up_w, grad_down_w = place_sums(
        total, swap(total), here, wide_row, quarter, half // RING, width
    )
    grad_down_w = grad_down_w.reshape(hidden_part, width)
    return (
        layer_out[None],
        grad_input[None],
        sums_first[:part],
        grad_qkv_w,
        sums_first[part : part + qk_part],
        sums_second[part : part + kv_part],
        grad_out_w,
        sums_second[:part],
        grad_gate_w,
        grad_up_w,
        grad_down_w,
    )


def solution(mesh):
    devices = mesh.devices
    dp, ctx, fsdp = devices.shape
    fine = Mesh(devices.reshape(dp, RING, ctx // RING, fsdp), ("dp", "y", "x", "fsdp"))
    rows = P(("dp", "fsdp"), ("y", "x"), None)
    vec = P("fsdp")
    mat = P("fsdp", None)
    return jax.shard_map(
        per_device,
        mesh=fine,
        in_specs=(rows, vec, mat, vec, mat, vec, mat, mat, mat, rows),
        out_specs=(rows, rows, vec, mat, vec, vec, mat, vec, mat, mat, mat),
        check_vma=False,
    )
```
